32 devices in a mesh: groups: 1, dp: 16 (over z, y, x), mp: 2 (over core).
Axes of the slice: x: 2, y: 2, z: 4, core: 2. Of those that a mesh axis runs over, the one named last changes fastest.
Arguments:
- tokens: bfloat16 [6144, 8192], P(('groups', 'dp'), 'mp'), may hold values from -6 to 6
- cotangent: bfloat16 [6144, 8192], P(('groups', 'dp'), 'mp'), may hold values from -6 to 6
- lengths: int32 [16, 4], P(('groups', 'dp')), may hold values from 48 to 96, as said below
- up_first: bfloat16 [128, 4096], P('mp', 'dp'), may hold values from -0.75 to 0.75
- up_second: bfloat16 [128, 16384], P('mp', 'dp'), may hold values from -0.75 to 0.75
- down_first: bfloat16 [128, 16384], P('mp', 'dp'), may hold values from -0.375 to 0.375
- down_second: bfloat16 [128, 4096], P('mp', 'dp'), may hold values from -0.75 to 0.75
Outputs:
- input_grad: bfloat16 [6144, 8192], P(('groups', 'dp'), 'mp')
- grad_up_first: float32 [128, 4096], P(('groups', 'mp'), 'dp')
- grad_up_second: float32 [128, 16384], P(('groups', 'mp'), 'dp')
- grad_down_first: float32 [128, 16384], P(('groups', 'mp'), 'dp')
- grad_down_second: float32 [128, 4096], P(('groups', 'mp'), 'dp')
The draws below stay inside these ranges and needn't reach their ends.
Inputs may be any that keep to these rules, and one draw needn't show every extreme that they name: `lengths`: every microbatch has one segment of exactly 96 tokens.
All inputs are finite; a program needn't handle non-finite values.
Results may differ from the reference program's by a relative error of at most 0.019.
Values may be sent and summed in bfloat16 or wider, within the bound.
A program may use at most 192 MiB of HBM per device.

```python
import jax
import jax.numpy as jnp
from jax import lax

P_SIZE = 64
Q = 256
BLOCKS = 128
D = 8192
TOK_DEV = 384
SEGS = 4
SEG_MOST = 96
MICROS = 16
TOKENS = 6144


def draw_lengths(key, part):
    base = jax.random.fold_in(key, 17)
    first_key, second_key = jax.random.split(base)
    lowest = SEG_MOST - SEG_MOST // 2
    values = jax.random.randint(first_key, (MICROS, SEGS), lowest, SEG_MOST + 1)
    picked = jax.random.randint(second_key, (MICROS, 1), 0, SEGS)
    columns = jnp.arange(SEGS, dtype=jnp.int32)[None, :]
    return jnp.where(columns == picked, SEG_MOST, values).astype(jnp.int32)


def steps_of(key, dims, pieces, least, high):
    def one(position, shards_of):
        steps = jax.random.uniform(jax.random.fold_in(jax.random.fold_in(key, 6), position), (shards_of,), jnp.float32, least / len(pieces), high / len(pieces))
        return jnp.repeat(jnp.exp(steps), dims[position] // shards_of).reshape((-1,) + (1,) * (len(dims) - position - 1))

    factor_of = one(*pieces[0])
    for cut in pieces[1:]:
        factor_of = factor_of * one(*cut)
    return factor_of


def noise(key, shape, width, most, cuts=(), held_as=jnp.bfloat16):
    entries = width * jax.random.normal(key, shape, jnp.float32)
    if cuts:
        entries = entries * steps_of(key, shape, cuts, -0.22, 0.18)
    return jnp.clip(entries, -most, most).astype(held_as)


def setup_inputs(seed: int = 0, part: int = 0) -> dict:
    splits = jax.random.split(jax.random.key(seed), 8)
    part_keys = jax.random.split(jax.random.fold_in(splits[7], part), 8)
    return {
        "tokens": noise(part_keys[0], (TOKENS, D), 1.0, 6.0, ((0, 16), (1, 2))),
        "cotangent": noise(part_keys[1], (TOKENS, D), 1.0, 6.0, ((0, 16), (1, 2))),
        "lengths": draw_lengths(jax.random.fold_in(jax.random.fold_in(splits[7], part), 71), part),
        "up_first": noise(splits[3], (BLOCKS, P_SIZE * P_SIZE), P_SIZE ** -0.5, 0.75, ((0, 2), (1, 16))),
        "up_second": noise(splits[4], (BLOCKS, P_SIZE * Q), P_SIZE ** -0.5, 0.75, ((0, 2), (1, 16))),
        "down_first": noise(splits[5], (BLOCKS, Q * P_SIZE), Q ** -0.5, 0.375, ((0, 2), (1, 16))),
        "down_second": noise(splits[6], (BLOCKS, P_SIZE * P_SIZE), P_SIZE ** -0.5, 0.75, ((0, 2), (1, 16))),
    }


def smooth(values):
    return 0.5 * values * (1.0 + jnp.tanh(0.7978845608028654 * (values + 0.044715 * values * values * values)))

def token_scale(seg_lengths, count):
    ends = jnp.cumsum(seg_lengths)
    starts = ends - seg_lengths
    positions = jnp.arange(count, dtype=jnp.int32)[:, None]
    inside = (positions >= starts[None, :]) & (positions < ends[None, :])
    weights = SEG_MOST / seg_lengths.astype(jnp.float32)
    return lax.optimization_barrier(jnp.sum(jnp.where(inside, weights[None, :], jnp.zeros_like(weights)[None, :]), axis=1))

def to_mixed(values):
    count = values.shape[0]
    ratio = BLOCKS // P_SIZE
    return values.reshape(count, ratio, P_SIZE, P_SIZE).transpose(0, 3, 1, 2).reshape(count, BLOCKS, P_SIZE)

def from_mixed(values):
    count = values.shape[0]
    ratio = BLOCKS // P_SIZE
    return values.reshape(count, P_SIZE, ratio, P_SIZE).transpose(0, 2, 3, 1).reshape(count, BLOCKS, P_SIZE)

def rounded(values):
    return lax.optimization_barrier(values.astype(jnp.bfloat16)).astype(jnp.float32)

def reference(tokens, cotangent, lengths, up_first, up_second, down_first, down_second):
    single_float = jnp.float32
    brain_float_half = jnp.bfloat16
    wone = up_first.astype(single_float).reshape(BLOCKS, P_SIZE, P_SIZE)
    wtwo = up_second.astype(single_float).reshape(BLOCKS, P_SIZE, Q)
    third_weight = down_first.astype(single_float).reshape(BLOCKS, Q, P_SIZE)
    wfour = down_second.astype(single_float).reshape(BLOCKS, P_SIZE, P_SIZE)

    def step(totals, inputs):
        rows, cot_rows, seg_lengths = inputs
        blocked = rows.reshape(TOK_DEV, BLOCKS, P_SIZE).astype(single_float)
        first = jnp.einsum('tbp,bpj->tbj', blocked, wone).astype(brain_float_half)
        mixed_in = to_mixed(first).astype(single_float)
        pre_sum = jnp.einsum('tkm,kmq->tkq', mixed_in, wtwo)
        pre = pre_sum.astype(brain_float_half)
        gelu_activation = smooth(pre_sum).astype(brain_float_half).astype(single_float)
        narrow_rows = jnp.einsum('gxa,xad->gxd', gelu_activation, third_weight).astype(brain_float_half)
        mixed_out = from_mixed(narrow_rows).astype(single_float)
        scale = token_scale(seg_lengths, TOK_DEV)
        out_grad = (cot_rows.astype(single_float) * scale[:, None]).astype(brain_float_half).astype(single_float).reshape(TOK_DEV, BLOCKS, P_SIZE)
        g_four = jnp.einsum('tbj,tbq->bjq', mixed_out, out_grad)
        d_mixed_out = jnp.einsum('tbq,bjq->tbj', out_grad, wfour).astype(brain_float_half)
        narrow_gradient = to_mixed(d_mixed_out).astype(single_float)
        third_factor_gradient = jnp.einsum('aus,auf->usf', gelu_activation, narrow_gradient)
        activation_gradient = jnp.einsum('wez,ehz->weh', narrow_gradient, third_weight)
        unused, pullback = jax.vjp(smooth, pre.astype(single_float))
        d_pre = pullback(activation_gradient)[0].astype(brain_float_half).astype(single_float)
        g_two = jnp.einsum('tkm,tkq->kmq', mixed_in, d_pre)
        d_mixed_in = jnp.einsum('tkq,kmq->tkm', d_pre, wtwo).astype(brain_float_half)
        d_first = from_mixed(d_mixed_in).astype(single_float)
        g_one = jnp.einsum('tbp,tbj->bpj', blocked, d_first)
        input_rows = jnp.einsum('tbj,bpj->tbp', d_first, wone).astype(brain_float_half).reshape(TOK_DEV, D)
        parts = (g_one.reshape(BLOCKS, P_SIZE * P_SIZE), g_two.reshape(BLOCKS, P_SIZE * Q), third_factor_gradient.reshape(BLOCKS, Q * P_SIZE), g_four.reshape(BLOCKS, P_SIZE * P_SIZE))
        totals = tuple((total + rounded(piece) for total, piece in zip(totals, parts)))
        return (totals, input_rows)
    init = (jnp.zeros((BLOCKS, P_SIZE * P_SIZE), single_float), jnp.zeros((BLOCKS, P_SIZE * Q), single_float), jnp.zeros((BLOCKS, Q * P_SIZE), single_float), jnp.zeros((BLOCKS, P_SIZE * P_SIZE), single_float))
    totals, input_rows = lax.scan(step, init, (tokens.reshape(MICROS, TOK_DEV, D), cotangent.reshape(MICROS, TOK_DEV, D), lengths))
    return (input_rows.reshape(TOKENS, D), totals[0], totals[1], totals[2], totals[3])
```

```python
import jax
import jax.numpy as jnp
from jax import lax
from jax.sharding import PartitionSpec as P

P_SIZE = 64
Q = 256
SEG_MOST = 96


def smooth(values):
    return (
        0.5
        * values
        * (1.0 + jnp.tanh(0.7978845608028654 * (values + 0.044715 * values * values * values)))
    )


def token_scale(seg_lengths, count):
    order = jnp.arange(seg_lengths.shape[0], dtype=jnp.int32)
    ends = jnp.sum(
        jnp.where(order[None, :] <= order[:, None], seg_lengths[None, :], 0), axis=1
    )
    starts = ends - seg_lengths
    positions = jnp.arange(count, dtype=jnp.int32)[:, None]
    inside = (positions >= starts[None, :]) & (positions < ends[None, :])
    weights = SEG_MOST / seg_lengths.astype(jnp.float32)
    return jnp.sum(jnp.where(inside, weights[None, :], jnp.zeros_like(weights)[None, :]), axis=1)


def to_second(field, shares):
    row_count, inner, blocks = field.shape
    grouped = field.reshape(row_count, shares, inner // shares * blocks)
    moved = lax.all_to_all(grouped, "mp", split_axis=1, concat_axis=1, tiled=True)
    moved = moved.reshape(row_count, shares, inner // shares, blocks).transpose(0, 2, 1, 3)
    return moved.reshape(row_count, inner, blocks)


def to_first(field, shares):
    row_count, blocks, width = field.shape
    grouped = field.reshape(row_count, blocks // shares, shares, width).transpose(0, 2, 1, 3)
    grouped = grouped.reshape(row_count, shares, blocks // shares * width)
    moved = lax.all_to_all(grouped, "mp", split_axis=1, concat_axis=1, tiled=True)
    return moved.reshape(row_count, blocks, width)


def shards(tokens, cotangent, lengths, up_first, up_second, down_first, down_second):
    single_float = jnp.float32
    brain_float_half = jnp.bfloat16
    shares = lax.axis_size("mp")
    local_blocks = up_first.shape[0]
    row_count = tokens.shape[0]
    whole_one, whole_two, whole_three, whole_four = (
        lax.all_gather(up_first, "dp", axis=1, tiled=True),
        lax.all_gather(up_second, "dp", axis=1, tiled=True),
        lax.all_gather(down_first, "dp", axis=1, tiled=True),
        lax.all_gather(down_second, "dp", axis=1, tiled=True),
    )
    wone = whole_one.reshape(local_blocks, P_SIZE, P_SIZE)
    wtwo = whole_two.reshape(local_blocks, P_SIZE, Q)
    third_weight = whole_three.reshape(local_blocks, Q, P_SIZE)
    wfour = whole_four.reshape(local_blocks, P_SIZE, P_SIZE)
    blocked = tokens.reshape(row_count, local_blocks, P_SIZE)
    first = jnp.einsum("tmp,mpj->tjm", blocked, wone, preferred_element_type=single_float).astype(
        brain_float_half
    )
    mixed_in = to_second(first, shares)
    pre_sum = jnp.einsum("tkm,kmq->tkq", mixed_in, wtwo, preferred_element_type=single_float)
    pre = pre_sum.astype(brain_float_half)
    gelu_activation = smooth(pre_sum).astype(brain_float_half)
    narrow_rows = jnp.einsum(
        "gxa,xad->gxd", gelu_activation, third_weight, preferred_element_type=single_float
    ).astype(brain_float_half)
    mixed_out = to_first(narrow_rows, shares)
    scale = token_scale(lengths[0], row_count)
    out_grad = (
        (cotangent.astype(single_float) * scale[:, None])
        .astype(brain_float_half)
        .reshape(row_count, local_blocks, P_SIZE)
    )
    g_four = jnp.einsum(
        "tjm,tmq->mjq", mixed_out, out_grad, preferred_element_type=single_float
    ).reshape(local_blocks, P_SIZE * P_SIZE)
    d_mixed_out = jnp.einsum(
        "tmq,mjq->tjm", out_grad, wfour, preferred_element_type=single_float
    ).astype(brain_float_half)
    narrow_gradient = to_second(d_mixed_out, shares)
    third_factor_gradient = jnp.einsum(
        "aus,auf->usf", gelu_activation, narrow_gradient, preferred_element_type=single_float
    ).reshape(local_blocks, Q * P_SIZE)
    activation_gradient = jnp.einsum(
        "wez,ehz->weh", narrow_gradient, third_weight, preferred_element_type=single_float
    )
    unused, pullback = jax.vjp(smooth, pre.astype(single_float))
    d_pre = pullback(activation_gradient)[0].astype(brain_float_half)
    g_two = jnp.einsum(
        "tkm,tkq->kmq", mixed_in, d_pre, preferred_element_type=single_float
    ).reshape(local_blocks, P_SIZE * Q)
    d_mixed_in = jnp.einsum(
        "tkq,kmq->tkm", d_pre, wtwo, preferred_element_type=single_float
    ).astype(brain_float_half)
    d_first = to_first(d_mixed_in, shares)
    g_one = jnp.einsum(
        "tmp,tjm->mpj", blocked, d_first, preferred_element_type=single_float
    ).reshape(local_blocks, P_SIZE * P_SIZE)
    input_grad = jnp.einsum(
        "tjm,mpj->tmp", d_first, wone, preferred_element_type=single_float
    ).astype(brain_float_half)
    input_grad = input_grad.reshape(row_count, local_blocks * P_SIZE)
    g_one, g_two, third_factor_gradient, g_four = (
        lax.psum_scatter(g_one.astype(jnp.bfloat16), "dp", scatter_dimension=1, tiled=True).astype(
            jnp.float32
        ),
        lax.psum_scatter(g_two.astype(jnp.bfloat16), "dp", scatter_dimension=1, tiled=True).astype(
            jnp.float32
        ),
        lax.psum_scatter(
            third_factor_gradient.astype(jnp.bfloat16), "dp", scatter_dimension=1, tiled=True
        ).astype(jnp.float32),
        lax.psum_scatter(g_four.astype(jnp.bfloat16), "dp", scatter_dimension=1, tiled=True).astype(
            jnp.float32
        ),
    )
    return (input_grad, g_one, g_two, third_factor_gradient, g_four)


def solution(mesh):
    in_specs = (
        P(("groups", "dp"), "mp"),
        P(("groups", "dp"), "mp"),
        P(("groups", "dp"), None),
        P("mp", "dp"),
        P("mp", "dp"),
        P("mp", "dp"),
        P("mp", "dp"),
    )
    out_specs = (
        P(("groups", "dp"), "mp"),
        P(("groups", "mp"), "dp"),
        P(("groups", "mp"), "dp"),
        P(("groups", "mp"), "dp"),
        P(("groups", "mp"), "dp"),
    )
    return jax.shard_map(shards, mesh=mesh, in_specs=in_specs, out_specs=out_specs, check_vma=False)
```

```python
import jax
import jax.numpy as jnp
from jax import lax
from jax.sharding import PartitionSpec as P

P_SIZE = 64
Q = 256
SEG_MOST = 96


def smooth(values):
    return (
        0.5
        * values
        * (1.0 + jnp.tanh(0.7978845608028654 * (values + 0.044715 * values * values * values)))
    )


def token_scale(seg_lengths, count):
    order = jnp.arange(seg_lengths.shape[0], dtype=jnp.int32)
    ends = jnp.sum(
        jnp.where(order[None, :] <= order[:, None], seg_lengths[None, :], 0), axis=1
    )
    starts = ends - seg_lengths
    positions = jnp.arange(count, dtype=jnp.int32)[:, None]
    inside = (positions >= starts[None, :]) & (positions < ends[None, :])
    weights = SEG_MOST / seg_lengths.astype(jnp.float32)
    return jnp.sum(jnp.where(inside, weights[None, :], jnp.zeros_like(weights)[None, :]), axis=1)


def to_second(field, shares):
    row_count, inner, blocks = field.shape
    grouped = field.reshape(row_count, shares, inner // shares * blocks)
    moved = lax.all_to_all(grouped, "mp", split_axis=1, concat_axis=1, tiled=True)
    moved = moved.reshape(row_count, shares, inner // shares, blocks).transpose(0, 2, 1, 3)
    return moved.reshape(row_count, inner, blocks)


def to_first(field, shares):
    row_count, blocks, width = field.shape
    grouped = field.reshape(row_count, blocks // shares, shares, width).transpose(0, 2, 1, 3)
    grouped = grouped.reshape(row_count, shares, blocks // shares * width)
    moved = lax.all_to_all(grouped, "mp", split_axis=1, concat_axis=1, tiled=True)
    return moved.reshape(row_count, blocks, width)


def shards(tokens, cotangent, lengths, up_first, up_second, down_first, down_second):
    single_float = jnp.float32
    brain_float_half = jnp.bfloat16
    shares = lax.axis_size("mp")
    local_blocks = up_first.shape[0]
    row_count = tokens.shape[0]
    parts = lax.axis_size("dp")

    def gathered(left, right):
        width = left.shape[1]
        whole = lax.all_gather(jnp.concatenate([left, right], axis=1), "dp", axis=0)
        return tuple(
            piece.transpose(1, 0, 2).reshape(local_blocks, -1)
            for piece in (whole[:, :, :width], whole[:, :, width:])
        )

    whole_one, whole_four = gathered(up_first, down_second)
    whole_two, whole_three = gathered(up_second, down_first)
    wone = whole_one.reshape(local_blocks, P_SIZE, P_SIZE)
    wtwo = whole_two.reshape(local_blocks, P_SIZE, Q)
    third_weight = whole_three.reshape(local_blocks, Q, P_SIZE)
    wfour = whole_four.reshape(local_blocks, P_SIZE, P_SIZE)
    blocked = tokens.reshape(row_count, local_blocks, P_SIZE)
    first = jnp.einsum("tmp,mpj->tjm", blocked, wone, preferred_element_type=single_float).astype(
        brain_float_half
    )
    mixed_in = to_second(first, shares)
    pre_sum = jnp.einsum("tkm,kmq->tkq", mixed_in, wtwo, preferred_element_type=single_float)
    pre = pre_sum.astype(brain_float_half)
    gelu_activation = smooth(pre_sum).astype(brain_float_half)
    narrow_rows = jnp.einsum(
        "gxa,xad->gxd", gelu_activation, third_weight, preferred_element_type=single_float
    ).astype(brain_float_half)
    mixed_out = to_first(narrow_rows, shares)
    scale = token_scale(lengths[0], row_count)
    out_grad = (
        (cotangent.astype(single_float) * scale[:, None])
        .astype(brain_float_half)
        .reshape(row_count, local_blocks, P_SIZE)
    )
    g_four = jnp.einsum(
        "tjm,tmq->mjq", mixed_out, out_grad, preferred_element_type=single_float
    ).reshape(local_blocks, P_SIZE * P_SIZE)
    d_mixed_out = jnp.einsum(
        "tmq,mjq->tjm", out_grad, wfour, preferred_element_type=single_float
    ).astype(brain_float_half)
    narrow_gradient = to_second(d_mixed_out, shares)
    third_factor_gradient = jnp.einsum(
        "aus,auf->usf", gelu_activation, narrow_gradient, preferred_element_type=single_float
    ).reshape(local_blocks, Q * P_SIZE)
    activation_gradient = jnp.einsum(
        "wez,ehz->weh", narrow_gradient, third_weight, preferred_element_type=single_float
    )
    unused, pullback = jax.vjp(smooth, pre.astype(single_float))
    d_pre = pullback(activation_gradient)[0].astype(brain_float_half)
    g_two = jnp.einsum(
        "tkm,tkq->kmq", mixed_in, d_pre, preferred_element_type=single_float
    ).reshape(local_blocks, P_SIZE * Q)
    d_mixed_in = jnp.einsum(
        "tkq,kmq->tkm", d_pre, wtwo, preferred_element_type=single_float
    ).astype(brain_float_half)
    d_first = to_first(d_mixed_in, shares)
    g_one = jnp.einsum(
        "tmp,tjm->mpj", blocked, d_first, preferred_element_type=single_float
    ).reshape(local_blocks, P_SIZE * P_SIZE)
    input_grad = jnp.einsum(
        "tjm,mpj->tmp", d_first, wone, preferred_element_type=single_float
    ).astype(brain_float_half)
    input_grad = input_grad.reshape(row_count, local_blocks * P_SIZE)
    pieces = [
        piece.astype(brain_float_half).reshape(local_blocks, parts, -1).transpose(1, 0, 2)
        for piece in (g_one, g_two, third_factor_gradient, g_four)
    ]
    summed = lax.psum_scatter(
        jnp.concatenate(pieces, axis=2), "dp", scatter_dimension=0, tiled=False
    ).astype(single_float)
    cuts, at = [], 0
    for piece in pieces:
        cuts.append(summed[:, at : at + piece.shape[2]])
        at += piece.shape[2]
    g_one, g_two, third_factor_gradient, g_four = cuts
    return (input_grad, g_one, g_two, third_factor_gradient, g_four)


def solution(mesh):
    in_specs = (
        P(("groups", "dp"), "mp"),
        P(("groups", "dp"), "mp"),
        P(("groups", "dp"), None),
        P("mp", "dp"),
        P("mp", "dp"),
        P("mp", "dp"),
        P("mp", "dp"),
    )
    out_specs = (
        P(("groups", "dp"), "mp"),
        P(("groups", "mp"), "dp"),
        P(("groups", "mp"), "dp"),
        P(("groups", "mp"), "dp"),
        P(("groups", "mp"), "dp"),
    )
    return jax.shard_map(shards, mesh=mesh, in_specs=in_specs, out_specs=out_specs, check_vma=False)
```

```python
import jax
import jax.numpy as jnp
from jax import lax
from jax.experimental import pallas as pl
from jax.experimental.pallas import tpu as pltpu
from jax.sharding import PartitionSpec as P

P_SIZE = 64
Q = 256
SEG_MOST = 96


ROOT = 0.7978845608028654
CUBIC = 0.044715


def token_scale(seg_lengths, count):
    order = jnp.arange(seg_lengths.shape[0], dtype=jnp.int32)
    ends = jnp.sum(
        jnp.where(order[None, :] <= order[:, None], seg_lengths[None, :], 0), axis=1
    )
    starts = ends - seg_lengths
    positions = jnp.arange(count, dtype=jnp.int32)[:, None]
    inside = (positions >= starts[None, :]) & (positions < ends[None, :])
    weights = SEG_MOST / seg_lengths.astype(jnp.float32)
    return jnp.sum(jnp.where(inside, weights[None, :], jnp.zeros_like(weights)[None, :]), axis=1)


def exchange(field, shares):
    field = field.reshape(shares, -1, *field.shape[1:])
    return lax.all_to_all(field, "mp", split_axis=0, concat_axis=0, tiled=True)


def exchange_back(field):
    moved = lax.all_to_all(field, "mp", split_axis=0, concat_axis=0, tiled=True)
    return moved.reshape(-1, *moved.shape[2:])


def middle(mixed_ref, grad_ref, two_ref, three_ref, narrow_ref, d_mixed_ref, g_two_ref, g_three_ref):
    dims = (((1,), (0,)), ((), ()))
    across = (((1,), (1,)), ((), ()))

    def dot(left, right, how=dims):
        return lax.dot_general(left, right, how, preferred_element_type=jnp.float32)

    for h in range(mixed_ref.shape[0]):
        mixed, grad = mixed_ref[h, 0], grad_ref[h, 0]
        two, three = two_ref[h], three_ref[h]
        pre = dot(two.T, mixed)
        square = pre * pre
        wave = jnp.tanh(pre * (ROOT + (ROOT * CUBIC) * square))
        half = 0.5 + 0.5 * wave
        act = (pre * half).astype(jnp.bfloat16)
        narrow_ref[h, 0] = dot(three.T, act).astype(jnp.bfloat16)
        g_three_ref[h] = dot(act, grad, across).astype(jnp.bfloat16)
        slope = half + (pre * (ROOT + (3.0 * ROOT * CUBIC) * square)) * (0.5 - 0.5 * wave * wave)
        d_pre = (slope * dot(three, grad)).astype(jnp.bfloat16)
        d_mixed_ref[h, 0] = dot(two, d_pre).astype(jnp.bfloat16)
        g_two_ref[h] = dot(mixed, d_pre, across).astype(jnp.bfloat16)


def middle_call(mixed, grad, two, three):
    shares, steps, inner, tokens = mixed.shape
    token_spec = pl.BlockSpec((shares, 1, inner, tokens), lambda j: (0, j, 0, 0))

    def weight_spec(array):
        return pl.BlockSpec((shares, *array.shape[1:]), lambda j: (j, 0, 0))

    return pl.pallas_call(
        middle,
        grid=(steps,),
        in_specs=[token_spec, token_spec, weight_spec(two), weight_spec(three)],
        out_specs=[token_spec, token_spec, weight_spec(two), weight_spec(three)],
        out_shape=[
            jax.ShapeDtypeStruct(array.shape, jnp.bfloat16) for array in (mixed, grad, two, three)
        ],
        compiler_params=pltpu.CompilerParams(vmem_limit_bytes=32 * 2**20),
        cost_estimate=pl.CostEstimate(
            flops=12 * two.size * tokens,
            bytes_accessed=4 * (mixed.size + grad.size + two.size + three.size),
            transcendentals=two.size // inner * tokens,
        ),
    )(mixed, grad, two, three)


def shards(tokens, cotangent, lengths, up_first, up_second, down_first, down_second):
    single_float = jnp.float32
    brain_float_half = jnp.bfloat16
    shares = lax.axis_size("mp")
    local_blocks = up_first.shape[0]
    row_count = tokens.shape[0]
    parts = lax.axis_size("dp")

    factors = (up_first, up_second, down_first, down_second)
    whole = lax.all_gather(jnp.concatenate(factors, axis=1), "dp", axis=0)
    unpacked, at = [], 0
    for factor in factors:
        piece = whole[:, :, at : at + factor.shape[1]]
        unpacked.append(piece.transpose(1, 0, 2).reshape(local_blocks, -1))
        at += factor.shape[1]
    whole_one, whole_two, whole_three, whole_four = unpacked
    wone = whole_one.reshape(local_blocks, P_SIZE, P_SIZE)
    wtwo = whole_two.reshape(local_blocks, P_SIZE, Q)
    third_weight = whole_three.reshape(local_blocks, Q, P_SIZE)
    wfour = whole_four.reshape(local_blocks, P_SIZE, P_SIZE)
    blocked = tokens.reshape(row_count, local_blocks, P_SIZE)
    first = jnp.einsum("tmp,mpj->jmt", blocked, wone, preferred_element_type=single_float).astype(
        brain_float_half
    )
    mixed_in = exchange(first, shares)
    scale = token_scale(lengths[0], row_count)
    out_grad = (
        (cotangent.astype(single_float) * scale[:, None])
        .astype(brain_float_half)
        .reshape(row_count, local_blocks, P_SIZE)
    )
    d_mixed_out = jnp.einsum(
        "tmq,mjq->jmt", out_grad, wfour, preferred_element_type=single_float
    ).astype(brain_float_half)
    narrow_gradient = exchange(d_mixed_out, shares)
    narrow, d_mixed_in, g_two, g_three = middle_call(mixed_in, narrow_gradient, wtwo, third_weight)
    mixed_out = exchange_back(narrow)
    d_first = exchange_back(d_mixed_in)
    g_four = jnp.einsum("jmt,tmq->mjq", mixed_out, out_grad, preferred_element_type=single_float)
    g_one = jnp.einsum("tmp,jmt->mpj", blocked, d_first, preferred_element_type=single_float)
    input_grad = jnp.einsum(
        "jmt,mpj->tmp", d_first, wone, preferred_element_type=single_float
    ).astype(brain_float_half)
    input_grad = input_grad.reshape(row_count, local_blocks * P_SIZE)
    pieces = [
        piece.astype(brain_float_half).reshape(local_blocks, parts, -1).transpose(1, 0, 2)
        for piece in (g_one, g_two, g_three, g_four)
    ]
    summed = lax.psum_scatter(
        jnp.concatenate(pieces, axis=2), "dp", scatter_dimension=0, tiled=False
    ).astype(single_float)
    cuts, at = [], 0
    for piece in pieces:
        cuts.append(summed[:, at : at + piece.shape[2]])
        at += piece.shape[2]
    g_one, g_two, g_three, g_four = cuts
    return (input_grad, g_one, g_two, g_three, g_four)


def solution(mesh):
    in_specs = (
        P(("groups", "dp"), "mp"),
        P(("groups", "dp"), "mp"),
        P(("groups", "dp"), None),
        P("mp", "dp"),
        P("mp", "dp"),
        P("mp", "dp"),
        P("mp", "dp"),
    )
    out_specs = (
        P(("groups", "dp"), "mp"),
        P(("groups", "mp"), "dp"),
        P(("groups", "mp"), "dp"),
        P(("groups", "mp"), "dp"),
        P(("groups", "mp"), "dp"),
    )
    return jax.shard_map(shards, mesh=mesh, in_specs=in_specs, out_specs=out_specs, check_vma=False)
```

```python
import jax
import jax.numpy as jnp
from jax import lax
from jax.experimental import pallas as pl
from jax.experimental.pallas import tpu as pltpu
from jax.sharding import PartitionSpec as P

P_SIZE = 64
Q = 256
SEG_MOST = 96


ROOT = 0.7978845608028654
CUBIC = 0.044715


def token_scale(seg_lengths, count):
    order = jnp.arange(seg_lengths.shape[0], dtype=jnp.int32)
    ends = jnp.sum(
        jnp.where(order[None, :] <= order[:, None], seg_lengths[None, :], 0), axis=1
    )
    starts = ends - seg_lengths
    positions = jnp.arange(count, dtype=jnp.int32)[:, None]
    inside = (positions >= starts[None, :]) & (positions < ends[None, :])
    weights = SEG_MOST / seg_lengths.astype(jnp.float32)
    return jnp.sum(jnp.where(inside, weights[None, :], jnp.zeros_like(weights)[None, :]), axis=1)


def exchange(field, shares):
    field = field.reshape(shares, -1, *field.shape[1:])
    return lax.all_to_all(field, "mp", split_axis=0, concat_axis=0, tiled=True)


def exchange_back(field):
    moved = lax.all_to_all(field, "mp", split_axis=0, concat_axis=0, tiled=True)
    return moved.reshape(-1, *moved.shape[2:])


def middle(mixed_ref, grad_ref, two_ref, three_ref, narrow_ref, d_mixed_ref, g_two_ref, g_three_ref):
    dims = (((1,), (0,)), ((), ()))
    across = (((1,), (1,)), ((), ()))

    def dot(left, right, how=dims):
        return lax.dot_general(left, right, how, preferred_element_type=jnp.float32)

    for h in range(mixed_ref.shape[0]):
        mixed, grad = mixed_ref[h, 0], grad_ref[h, 0]
        two, three = two_ref[h], three_ref[h]
        pre = dot(two.T, mixed)
        square = pre * pre
        wave = jnp.tanh(pre * (ROOT + (ROOT * CUBIC) * square))
        half = 0.5 + 0.5 * wave
        act = (pre * half).astype(jnp.bfloat16)
        narrow_ref[h, 0] = dot(three.T, act).astype(jnp.bfloat16)
        g_three_ref[h] = dot(act, grad, across).astype(jnp.bfloat16)
        slope = half + (pre * (ROOT + (3.0 * ROOT * CUBIC) * square)) * (0.5 - 0.5 * wave * wave)
        d_pre = (slope * dot(three, grad)).astype(jnp.bfloat16)
        d_mixed_ref[h, 0] = dot(two, d_pre).astype(jnp.bfloat16)
        g_two_ref[h] = dot(mixed, d_pre, across).astype(jnp.bfloat16)


def middle_call(mixed, grad, two, three):
    shares, steps, inner, tokens = mixed.shape
    token_spec = pl.BlockSpec((shares, 1, inner, tokens), lambda j: (0, j, 0, 0))

    def weight_spec(array):
        return pl.BlockSpec((shares, *array.shape[1:]), lambda j: (j, 0, 0))

    return pl.pallas_call(
        middle,
        grid=(steps,),
        in_specs=[token_spec, token_spec, weight_spec(two), weight_spec(three)],
        out_specs=[token_spec, token_spec, weight_spec(two), weight_spec(three)],
        out_shape=[
            jax.ShapeDtypeStruct(array.shape, jnp.bfloat16) for array in (mixed, grad, two, three)
        ],
        compiler_params=pltpu.CompilerParams(vmem_limit_bytes=32 * 2**20),
        cost_estimate=pl.CostEstimate(
            flops=12 * two.size * tokens,
            bytes_accessed=4 * (mixed.size + grad.size + two.size + three.size),
            transcendentals=two.size // inner * tokens,
        ),
    )(mixed, grad, two, three)


def shards(tokens, cotangent, lengths, up_first, up_second, down_first, down_second):
    single_float = jnp.float32
    brain_float_half = jnp.bfloat16
    shares = lax.axis_size("mp")
    local_blocks = up_first.shape[0]
    row_count = tokens.shape[0]
    parts = lax.axis_size("dp")

    factors = (up_first, up_second, down_first, down_second)
    whole = lax.all_gather(jnp.concatenate(factors, axis=1), "dp", axis=0)
    unpacked, at = [], 0
    for factor in factors:
        piece = whole[:, :, at : at + factor.shape[1]]
        unpacked.append(piece.transpose(1, 0, 2).reshape(local_blocks, -1))
        at += factor.shape[1]
    whole_one, whole_two, whole_three, whole_four = unpacked
    wone = whole_one.reshape(local_blocks, P_SIZE, P_SIZE)
    wtwo = whole_two.reshape(local_blocks, P_SIZE, Q)
    third_weight = whole_three.reshape(local_blocks, Q, P_SIZE)
    wfour = whole_four.reshape(local_blocks, P_SIZE, P_SIZE)
    blocked = tokens.reshape(row_count, local_blocks, P_SIZE)
    first = jnp.einsum("tmp,mpj->jmt", blocked, wone, preferred_element_type=single_float).astype(
        brain_float_half
    )
    mixed_in = exchange(first, shares)
    scale = token_scale(lengths[0], row_count)
    out_grad = (
        (cotangent.astype(single_float) * scale[:, None])
        .astype(brain_float_half)
        .reshape(row_count, local_blocks, P_SIZE)
    )
    d_mixed_out = jnp.einsum(
        "tmq,mjq->jmt", out_grad, wfour, preferred_element_type=single_float
    ).astype(brain_float_half)
    narrow_gradient = exchange(d_mixed_out, shares)
    narrow, d_mixed_in, g_two, g_three = middle_call(mixed_in, narrow_gradient, wtwo, third_weight)

    def packed(*gradients):
        pieces = [
            piece.astype(brain_float_half).reshape(local_blocks, parts, -1).transpose(1, 0, 2)
            for piece in gradients
        ]
        return jnp.concatenate(pieces, axis=2)

    large, narrow, d_mixed_in = lax.optimization_barrier(
        (packed(g_two, g_three), narrow, d_mixed_in)
    )
    large = lax.psum_scatter(large, "dp", scatter_dimension=0, tiled=False)
    mixed_out = exchange_back(narrow)
    d_first = exchange_back(d_mixed_in)
    g_four = jnp.einsum("jmt,tmq->mjq", mixed_out, out_grad, preferred_element_type=single_float)
    g_one = jnp.einsum("tmp,jmt->mpj", blocked, d_first, preferred_element_type=single_float)
    input_grad = jnp.einsum(
        "jmt,mpj->tmp", d_first, wone, preferred_element_type=single_float
    ).astype(brain_float_half)
    input_grad = input_grad.reshape(row_count, local_blocks * P_SIZE)
    small = lax.all_to_all(packed(g_one, g_four), "dp", split_axis=0, concat_axis=0, tiled=True)
    small = jnp.sum(small.astype(single_float), axis=0)
    g_one, g_four = jnp.split(small, 2, axis=1)
    g_two, g_three = jnp.split(large.astype(single_float), 2, axis=1)
    return (input_grad, g_one, g_two, g_three, g_four)


def solution(mesh):
    in_specs = (
        P(("groups", "dp"), "mp"),
        P(("groups", "dp"), "mp"),
        P(("groups", "dp"), None),
        P("mp", "dp"),
        P("mp", "dp"),
        P("mp", "dp"),
        P("mp", "dp"),
    )
    out_specs = (
        P(("groups", "dp"), "mp"),
        P(("groups", "mp"), "dp"),
        P(("groups", "mp"), "dp"),
        P(("groups", "mp"), "dp"),
        P(("groups", "mp"), "dp"),
    )
    return jax.shard_map(shards, mesh=mesh, in_specs=in_specs, out_specs=out_specs, check_vma=False)
```
